32 devices in a mesh: trial: 2 (over y), freq: 4 (over z), acc: 4 (over x, core).
Axes of the slice: x: 2, y: 2, z: 4, core: 2. Of those that a mesh axis runs over, the one named last changes fastest.
Arguments:
- spectrum: bfloat16 [2, 8192], P(None, ('trial', 'freq')), parts along dimension 1, may hold values from -6 to 6
- templates: bfloat16 [2, 200, 384], P(None, 'acc'), may hold values from -0.15625 to 0.15625
- offsets: int32 [200], P('acc'), may hold values from 0 to 127
Outputs:
- harmonic_sum: float32 [200, 8192], P(None, ('trial', 'freq', 'acc')), parts along dimension 1
The draws below stay inside these ranges and needn't reach their ends.
There are 2 independent parts, one for each index of `trial`. The reference program is written for one: setup_inputs(seed, part) draws one part's arguments, and reference() takes and returns one part's arrays. A program takes and returns all parts, laid end to end along the dimension named above; an argument that names none is the same for every part. Nothing has to cross between parts.
All inputs are finite; a program needn't handle non-finite values.
Results may differ from the reference program's by a relative error of at most 0.0033.
Values may be sent and summed in bfloat16 or wider, within the bound.
No kernel may reach another device: no remote copies, remote signals or barrier semaphores. Data moves between devices by JAX's collectives and lax.ppermute only.
A program may use at most 64 MiB of HBM per device.

```python
import jax
import jax.numpy as jnp
from jax import lax

Z = 200
K = 384
OFF = 128
H = 8
NF = 4096


def set_ends(values, own_key, low, top_value):
    dims = values.shape
    spot = [jax.random.randint(jax.random.fold_in(own_key, axis), (), 0, dims[axis]) for axis in range(len(dims))]
    values = values.at[tuple(spot)].set(low)
    longest = dims.index(max(dims))
    spot[longest] = (spot[longest] + 1) % dims[longest]
    return values.at[tuple(spot)].set(top_value)


def block_levels(stream_key, extent, split, least, largest):
    gain, own = 1.0, jax.random.fold_in(stream_key, 6)
    for axis_at, parts in split:
        draws = jnp.exp(jax.random.uniform(jax.random.fold_in(own, axis_at), (parts,), jnp.float32, least / len(split), largest / len(split)))
        gain = gain * jnp.repeat(draws, extent[axis_at] // parts).reshape([-1 if axis == axis_at else 1 for axis in range(len(extent))])
    return gain


def centred(rng, extent, scale, most, cuts=(), kind=jnp.bfloat16):
    array = jax.random.normal(rng, extent, jnp.float32) * scale
    if len(cuts) > 0:
        array = block_levels(rng, extent, cuts, -0.22, 0.18) * array
    return jnp.clip(array, min=-most, max=most).astype(kind)


def setup_inputs(seed: int = 0, part: int = 0) -> dict:
    key_list = jax.random.split(jax.random.key(seed), 4)
    own_keys = jax.random.split(jax.random.fold_in(key_list[3], part), 4)
    return {
        "spectrum": centred(own_keys[0], (2, NF), 1.0, 6.0, ((1, 4),)),
        "templates": centred(key_list[1], (2, Z, K), (4 * K) ** -0.5, 0.15625, ((1, 4),)),
        "offsets": set_ends(jax.random.randint(key_list[2], (Z,), 0, OFF), jax.random.fold_in(key_list[2], 1), 0, OFF - 1).astype(jnp.int32),
    }


def shifted_templates(templates, offsets, width):
    def place_row(template_row, start_col):
        zero_row = jnp.zeros((2, width), templates.dtype)
        return lax.dynamic_update_slice(zero_row, template_row, (jnp.int32(0), start_col))

    return jax.vmap(place_row, in_axes=(1, 0), out_axes=1)(templates, offsets.astype(jnp.int32))


def conv_kernel(shifted):
    real_part = shifted[0]
    imag_part = shifted[1]
    upper = jnp.stack([real_part, -imag_part], axis=1)
    lower = jnp.stack([imag_part, real_part], axis=1)
    return jnp.concatenate([upper, lower], axis=0)


def correlate_power(kernel, line, stride, out_len):
    product = lax.conv_general_dilated(line[None], kernel, (stride,), "VALID", dimension_numbers=("NCH", "OIH", "NCH"), preferred_element_type=jnp.float32)[0]
    product = product[:, :out_len]
    half_rows = kernel.shape[0] // 2
    real_out = product[:half_rows]
    imag_out = product[half_rows:]
    return (real_out * real_out + imag_out * imag_out).astype(jnp.bfloat16)


def harmonic_rows(harmonic):
    centre = Z // 2
    row_low = centre - centre // harmonic
    row_high = centre + (Z - 1 - centre) // harmonic
    return row_low, row_high - row_low + 1, centre - harmonic * (centre // harmonic)


def reference(spectrum, templates, offsets):
    total_bins = spectrum.shape[1]
    window_width = K + OFF
    padded = jnp.pad(spectrum, ((0, 0), (0, window_width)))
    kernel = conv_kernel(shifted_templates(templates, offsets, window_width))
    full_plane = correlate_power(kernel, padded, 1, total_bins)
    result = jnp.zeros((Z, total_bins), jnp.float32)
    for harmonic in range(1, H + 1):
        row_low, row_count, row_first = harmonic_rows(harmonic)
        row_block = full_plane[row_first:row_first + harmonic * (row_count - 1) + 1:harmonic]
        picked = row_block[:, ::harmonic].astype(jnp.float32)
        picked = jnp.pad(picked, ((row_low, Z - row_low - row_count), (0, total_bins - picked.shape[1])))
        result = result + picked
    return result
```

```python
import functools

import jax
import jax.numpy as jnp
from jax import lax
from jax.experimental import pallas as pl
from jax.experimental.pallas import tpu as pltpu
from jax.sharding import PartitionSpec as P

K = 384
OFF = 128
H = 8
LANES = 128
WIDTH = K + OFF
NT = (((1,), (1,)), ((), ()))
VMEM = pl.BlockSpec(memory_space=pltpu.VMEM)


def round_up(value, step):
    return (value + step - 1) // step * step


def row_blocks(rows):
    centre = rows // 2
    blocks = []
    for harmonic in range(1, H + 1):
        low = centre - centre // harmonic
        end = centre + (rows - 1 - centre) // harmonic + 1
        start = low // 16 * 16
        blocks.append((start, round_up(end, 16) - start))
    return blocks


def lane_gather(values, index):
    return jnp.take_along_axis(values, index, axis=1, mode="promise_in_bounds")


def shift_kernel(offsets_ref, templates_ref, out_ref):
    rows = templates_ref.shape[1]
    padded = out_ref.shape[1]
    taps = templates_ref.shape[2] // LANES
    spot = lax.broadcasted_iota(jnp.int32, (padded, rows), 0) == lax.broadcasted_iota(jnp.int32, (padded, rows), 1)
    offset = jnp.sum(jnp.where(spot, offsets_ref[...].astype(jnp.float32), 0.0), axis=1, keepdims=True)
    offset = jnp.broadcast_to(offset.astype(jnp.int32), (padded, LANES))
    lane = lax.broadcasted_iota(jnp.int32, (padded, LANES), 1)
    index = (lane - offset) & (LANES - 1)
    stays = lane >= offset
    for part in range(2):
        before = jnp.zeros((padded, LANES), jnp.float32)
        for tile in range(taps + 1):
            if tile < taps:
                values = templates_ref[part, :, tile * LANES : (tile + 1) * LANES].astype(jnp.float32)
                values = jnp.concatenate([values, jnp.zeros((padded - rows, LANES), jnp.float32)], axis=0)
                turned = lane_gather(values, index)
            else:
                turned = jnp.zeros((padded, LANES), jnp.float32)
            placed = jnp.where(stays, turned, before)
            out_ref[part, :, tile * LANES : (tile + 1) * LANES] = placed.astype(jnp.bfloat16)
            before = turned


def shift_templates(offsets, templates):
    parts, rows, _ = templates.shape
    return pl.pallas_call(
        shift_kernel,
        out_shape=jax.ShapeDtypeStruct((parts, round_up(rows, 16), WIDTH), jnp.bfloat16),
        in_specs=[VMEM, VMEM],
        out_specs=VMEM,
        name="shift_templates",
    )(offsets.reshape(1, rows), templates)


def harmonic_kernel(*refs, n_slabs, masks, shard_rows, rows):
    slabs = refs[:n_slabs]
    shards = refs[n_slabs : n_slabs + len(masks)]
    out_ref, line, windows, taps, picked, total = refs[n_slabs + len(masks) :]
    sub_bins = out_ref.shape[1]
    blocks_f = sub_bins // LANES
    window_tiles = WIDTH // LANES
    padded = shards[0].shape[1]
    slab_tiles = slabs[0].shape[1] // LANES
    filled = n_slabs * slab_tiles
    freq_index = lax.axis_index("freq")
    acc_index = lax.axis_index("acc")

    line[:, filled:, :] = jnp.zeros((2, line.shape[1] - filled, LANES), jnp.float32)
    for slot, slab in enumerate(slabs):
        values = slab[...].astype(jnp.float32)
        for tile in range(slab_tiles):
            for part in range(2):
                line[part, pl.ds(slot * slab_tiles + tile, 1), :] = values[part : part + 1, tile * LANES : (tile + 1) * LANES]

    for slot, shard in enumerate(shards):
        for part in range(2):
            taps[slot * padded : (slot + 1) * padded, part * WIDTH : (part + 1) * WIDTH] = shard[part]

    centre = rows // 2
    column = lax.broadcasted_iota(jnp.int32, (1, taps.shape[0]), 1)
    row_at = jnp.full(column.shape, -H * rows, jnp.int32)
    for slot, mask in enumerate(masks):
        inside = (column >= slot * padded) & (column < slot * padded + shard_rows)
        row_at = jnp.where(inside, (acc_index ^ mask) * shard_rows + column - slot * padded, row_at)
    blocks = row_blocks(rows)
    at = 0
    for harmonic in range(1, H + 1):
        start, count = blocks[harmonic - 1]
        row = lax.broadcasted_iota(jnp.int32, (count, taps.shape[0]), 0) + start
        choose = jnp.where(centre + harmonic * (row - centre) == row_at, 1.0, 0.0).astype(jnp.bfloat16)
        chosen = jnp.dot(choose, taps[...], preferred_element_type=jnp.float32).astype(jnp.bfloat16)
        picked[at : at + count, :] = chosen[:, :WIDTH]
        picked[at + count : at + 2 * count, :] = chosen[:, WIDTH:]
        at += 2 * count

    lane = lax.broadcasted_iota(jnp.int32, (16, LANES), 1)
    sublane = lax.broadcasted_iota(jnp.int32, (16, LANES), 0)
    total[...] = jnp.zeros_like(total)
    at = 0
    for harmonic in range(1, H + 1):
        place = lane + harmonic * sublane
        index = place & (LANES - 1)
        stays = place < LANES
        n_tiles = window_tiles + harmonic * blocks_f
        first = ((harmonic - 1) * freq_index * slab_tiles) + harmonic * acc_index * blocks_f
        first = jnp.minimum(first, filled)
        for part in range(2):
            turned = []
            for tile in range(n_tiles + 1):
                values = jnp.broadcast_to(line[part, pl.ds(first + tile, 1), :], (16, LANES))
                turned.append(lane_gather(values, index))
            base = [jnp.where(stays, turned[t], turned[t + 1]).astype(jnp.bfloat16) for t in range(n_tiles)]
            moved = {0: base}
            for group in range(LANES // 16):
                tile_by, lane_by = divmod(16 * harmonic * group, LANES)
                if lane_by not in moved:
                    rolled = [pltpu.roll(values, LANES - lane_by, 1) for values in base]
                    keep = lane < LANES - lane_by
                    moved[lane_by] = [jnp.where(keep, rolled[t], rolled[min(t + 1, n_tiles - 1)]) for t in range(n_tiles)]
                for block in range(blocks_f):
                    for tile in range(window_tiles):
                        row = block * LANES + 16 * group
                        windows[harmonic - 1, part, row : row + 16, tile * LANES : (tile + 1) * LANES] = moved[lane_by][
                            tile_by + harmonic * block + tile
                        ]
        start, count = blocks[harmonic - 1]
        chosen = picked[at : at + 2 * count, :]
        at += 2 * count
        with_real = lax.dot_general(chosen, windows[harmonic - 1, 0], NT, preferred_element_type=jnp.float32)
        with_imag = lax.dot_general(chosen, windows[harmonic - 1, 1], NT, preferred_element_type=jnp.float32)
        real = with_real[:count] - with_imag[count:]
        imag = with_imag[:count] + with_real[count:]
        power = (real * real + imag * imag).astype(jnp.bfloat16)
        total[start : start + count, :] += power.astype(jnp.float32)
    out_ref[...] = total[:rows, :]


def harmonic_sums(slabs, shards, masks, shard_rows, rows, sub_bins):
    padded = shards[0].shape[1]
    filled = len(slabs) * slabs[0].shape[1] // LANES
    beyond = WIDTH // LANES + H * (sub_bins // LANES) + 1
    picked_rows = 2 * sum(count for _, count in row_blocks(rows))
    return pl.pallas_call(
        functools.partial(harmonic_kernel, n_slabs=len(slabs), masks=masks, shard_rows=shard_rows, rows=rows),
        out_shape=jax.ShapeDtypeStruct((rows, sub_bins), jnp.float32),
        in_specs=[VMEM] * (len(slabs) + len(shards)),
        out_specs=VMEM,
        scratch_shapes=[
            pltpu.VMEM((2, filled + beyond, LANES), jnp.float32),
            pltpu.VMEM((H, 2, sub_bins, WIDTH), jnp.bfloat16),
            pltpu.VMEM((len(shards) * padded, 2 * WIDTH), jnp.bfloat16),
            pltpu.VMEM((picked_rows, WIDTH), jnp.bfloat16),
            pltpu.VMEM((round_up(rows, 16), sub_bins), jnp.float32),
        ],
        compiler_params=pltpu.CompilerParams(vmem_limit_bytes=32 << 20),
        name="harmonic_sums",
    )(*slabs, *shards)


def shards(spectrum, templates, offsets):
    freq_count = lax.axis_size("freq")
    acc_count = lax.axis_size("acc")
    shard_rows = templates.shape[1]
    slabs = [spectrum]
    for by in range(1, freq_count):
        slabs.append(lax.ppermute(spectrum, "freq", [(i, i - by) for i in range(by, freq_count)]))
    held = [shift_templates(offsets, templates)]
    masks = [0]
    step = acc_count // 2
    while step >= 1:
        pairs = [(i, i ^ step) for i in range(acc_count)]
        held = held + [lax.ppermute(shard, "acc", pairs) for shard in held]
        masks = masks + [mask ^ step for mask in masks]
        step //= 2
    return harmonic_sums(slabs, held, masks, shard_rows, acc_count * shard_rows, spectrum.shape[1] // acc_count)


def solution(mesh):
    return jax.shard_map(
        shards,
        mesh=mesh,
        in_specs=(P(None, ("trial", "freq")), P(None, "acc", None), P("acc")),
        out_specs=P(None, ("trial", "freq", "acc")),
        check_vma=False,
    )
```

```python
import functools

import jax
import jax.numpy as jnp
from jax import lax
from jax.experimental import pallas as pl
from jax.experimental.pallas import tpu as pltpu
from jax.sharding import PartitionSpec as P

K = 384
OFF = 128
H = 8
LANES = 128
WIDTH = K + OFF
NT = (((1,), (1,)), ((), ()))
VMEM = pl.BlockSpec(memory_space=pltpu.VMEM)


def round_up(value, step):
    return (value + step - 1) // step * step


def row_blocks(rows):
    centre = rows // 2
    blocks = []
    for harmonic in range(1, H + 1):
        low = centre - centre // harmonic
        end = centre + (rows - 1 - centre) // harmonic + 1
        start = low // 16 * 16
        blocks.append((start, round_up(end, 16) - start))
    return blocks


def lane_gather(values, index):
    return jnp.take_along_axis(values, index, axis=1, mode="promise_in_bounds")


def pick_kernel(*refs, masks, shard_rows, rows):
    held = refs[: len(masks)]
    picked, taps = refs[len(masks) :]
    acc_index = lax.axis_index("acc")
    both = 2 * shard_rows
    padded = taps.shape[0] // len(masks)
    tap_tiles = held[0].shape[2] // LANES
    lane = lax.broadcasted_iota(jnp.int32, (padded, LANES), 1)
    spot = lax.broadcasted_iota(jnp.int32, (padded, shard_rows), 0) // 2 == lax.broadcasted_iota(
        jnp.int32, (padded, shard_rows), 1
    )
    for slot in range(len(masks)):
        values = held[slot][...].reshape(both + 2, held[slot].shape[2]).astype(jnp.float32)
        packed = values[both : both + 1, :shard_rows]
        values = values[:both]
        values = jnp.concatenate([values, jnp.zeros((padded - both, values.shape[1]), jnp.float32)], axis=0)
        offset = jnp.sum(jnp.where(spot, packed, 0.0), axis=1, keepdims=True)
        offset = jnp.broadcast_to(offset.astype(jnp.int32), (padded, LANES))
        index = (lane - offset) & (LANES - 1)
        stays = lane >= offset
        before = jnp.zeros((padded, LANES), jnp.float32)
        for tile in range(tap_tiles + 1):
            if tile < tap_tiles:
                turned = lane_gather(values[:, tile * LANES : (tile + 1) * LANES], index)
            else:
                turned = jnp.zeros((padded, LANES), jnp.float32)
            placed = jnp.where(stays, turned, before).astype(jnp.bfloat16)
            taps[slot * padded : (slot + 1) * padded, tile * LANES : (tile + 1) * LANES] = placed
            before = turned

    centre = rows // 2
    column = lax.broadcasted_iota(jnp.int32, (1, taps.shape[0]), 1)
    row_at = jnp.full(column.shape, -2 * H * rows, jnp.int32)
    for slot, mask in enumerate(masks):
        inside = (column >= slot * padded) & (column < slot * padded + both)
        row_at = jnp.where(inside, (acc_index ^ mask) * both + column - slot * padded, row_at)
    at = 0
    for harmonic, (start, count) in enumerate(row_blocks(rows), 1):
        row = lax.broadcasted_iota(jnp.int32, (count, taps.shape[0]), 0) + start
        wanted = 2 * (centre + harmonic * (row - centre))
        for part in range(2):
            choose = jnp.where(wanted + part == row_at, 1.0, 0.0).astype(jnp.bfloat16)
            chosen = jnp.dot(choose, taps[...], preferred_element_type=jnp.float32)
            picked[at : at + count, :] = chosen.astype(jnp.bfloat16)
            at += count


def pick_templates(held, masks, rows):
    shard_rows = held[0].shape[0] - 1
    picked_rows = 2 * sum(count for _, count in row_blocks(rows))
    return pl.pallas_call(
        functools.partial(pick_kernel, masks=masks, shard_rows=shard_rows, rows=rows),
        out_shape=jax.ShapeDtypeStruct((picked_rows, WIDTH), jnp.bfloat16),
        in_specs=[VMEM] * len(masks),
        out_specs=VMEM,
        scratch_shapes=[pltpu.VMEM((len(masks) * round_up(2 * shard_rows, 16), WIDTH), jnp.bfloat16)],
        compiler_params=pltpu.CompilerParams(vmem_limit_bytes=16 << 20),
        name="pick_templates",
    )(*held)


def harmonic_kernel(*refs, n_slabs, rows):
    slabs = refs[:n_slabs]
    picked, out_ref, line, windows, total = refs[n_slabs:]
    sub_bins = out_ref.shape[1]
    blocks_f = sub_bins // LANES
    window_tiles = WIDTH // LANES
    slab_tiles = slabs[0].shape[1] // LANES
    filled = n_slabs * slab_tiles
    freq_index = lax.axis_index("freq")
    acc_index = lax.axis_index("acc")
    blocks = row_blocks(rows)

    line[:, filled:, :] = jnp.zeros((2, line.shape[1] - filled, LANES), jnp.float32)
    for slot, slab in enumerate(slabs[::-1]):
        values = slab[...].astype(jnp.float32)
        for tile in range(slab_tiles):
            for part in range(2):
                line[part, pl.ds(slot * slab_tiles + tile, 1), :] = values[part : part + 1, tile * LANES : (tile + 1) * LANES]

    lane = lax.broadcasted_iota(jnp.int32, (16, LANES), 1)
    sublane = lax.broadcasted_iota(jnp.int32, (16, LANES), 0)
    total[...] = jnp.zeros_like(total)
    at = 0
    for harmonic in range(1, H + 1):
        place = lane + harmonic * sublane
        index = place & (LANES - 1)
        stays = place < LANES
        n_tiles = window_tiles + harmonic * blocks_f
        first = ((harmonic - 1) * freq_index * slab_tiles) + harmonic * acc_index * blocks_f
        first = jnp.minimum(first, filled)
        for part in range(2):
            turned = []
            for tile in range(n_tiles + 1):
                values = jnp.broadcast_to(line[part, pl.ds(first + tile, 1), :], (16, LANES))
                turned.append(lane_gather(values, index))
            base = [jnp.where(stays, turned[t], turned[t + 1]).astype(jnp.bfloat16) for t in range(n_tiles)]
            moved = {0: base}
            for group in range(LANES // 16):
                tile_by, lane_by = divmod(16 * harmonic * group, LANES)
                if lane_by not in moved:
                    rolled = [pltpu.roll(values, LANES - lane_by, 1) for values in base]
                    keep = lane < LANES - lane_by
                    moved[lane_by] = [jnp.where(keep, rolled[t], rolled[min(t + 1, n_tiles - 1)]) for t in range(n_tiles)]
                for block in range(blocks_f):
                    for tile in range(window_tiles):
                        row = block * LANES + 16 * group
                        windows[harmonic - 1, part, row : row + 16, tile * LANES : (tile + 1) * LANES] = moved[lane_by][
                            tile_by + harmonic * block + tile
                        ]
        start, count = blocks[harmonic - 1]
        chosen = picked[at : at + 2 * count, :]
        at += 2 * count
        with_real = lax.dot_general(chosen, windows[harmonic - 1, 0], NT, preferred_element_type=jnp.float32)
        with_imag = lax.dot_general(chosen, windows[harmonic - 1, 1], NT, preferred_element_type=jnp.float32)
        real = with_real[:count] - with_imag[count:]
        imag = with_imag[:count] + with_real[count:]
        power = (real * real + imag * imag).astype(jnp.bfloat16)
        total[start : start + count, :] += power.astype(jnp.float32)
    out_ref[...] = total[:rows, :]


def harmonic_sums(slabs, picked, rows, sub_bins):
    filled = len(slabs) * slabs[0].shape[1] // LANES
    beyond = WIDTH // LANES + H * (sub_bins // LANES) + 1
    return pl.pallas_call(
        functools.partial(harmonic_kernel, n_slabs=len(slabs), rows=rows),
        out_shape=jax.ShapeDtypeStruct((rows, sub_bins), jnp.float32),
        in_specs=[VMEM] * (len(slabs) + 1),
        out_specs=VMEM,
        scratch_shapes=[
            pltpu.VMEM((2, filled + beyond, LANES), jnp.float32),
            pltpu.VMEM((H, 2, sub_bins, WIDTH), jnp.bfloat16),
            pltpu.VMEM((round_up(rows, 16), sub_bins), jnp.float32),
        ],
        compiler_params=pltpu.CompilerParams(vmem_limit_bytes=32 << 20),
        name="harmonic_sums",
    )(*slabs, picked)


def exchanged(values, step):
    count = lax.axis_size("acc")
    return [lax.ppermute(value, "acc", [(i, i ^ step) for i in range(count)]) for value in values]


def shards(spectrum, templates, offsets):
    freq_count = lax.axis_size("freq")
    acc_count = lax.axis_size("acc")
    held = jnp.transpose(templates, (1, 0, 2))
    rows = acc_count * held.shape[0]
    extra = jnp.pad(offsets.astype(jnp.bfloat16), (0, held.shape[2] - offsets.shape[0]))
    held = [jnp.concatenate([held, jnp.broadcast_to(extra, (1,) + held.shape[1:])], axis=0)]
    slabs = [
        lax.ppermute(spectrum, "freq", [(i, i - by) for i in range(by, freq_count)]) for by in range(freq_count - 1, 0, -1)
    ] + [spectrum]
    masks = list(range(acc_count))
    for mask in masks[:0:-1]:
        held = held[:1] + exchanged(held[:1], mask) + held[1:]
    picked = pick_templates(held, masks, rows)
    return harmonic_sums(slabs, picked, rows, spectrum.shape[1] // acc_count)


def solution(mesh):
    return jax.shard_map(
        shards,
        mesh=mesh,
        in_specs=(P(None, ("trial", "freq")), P(None, "acc", None), P("acc")),
        out_specs=P(None, ("trial", "freq", "acc")),
        check_vma=False,
    )
```

```python
import functools

import jax
import jax.numpy as jnp
from jax import lax
from jax.experimental import pallas as pl
from jax.experimental.pallas import tpu as pltpu
from jax.sharding import PartitionSpec as P

K = 384
OFF = 128
H = 8
LANES = 128
WIDTH = K + OFF
NT = (((1,), (1,)), ((), ()))
VMEM = pl.BlockSpec(memory_space=pltpu.VMEM)


def round_up(value, step):
    return (value + step - 1) // step * step


def row_blocks(rows):
    centre = rows // 2
    blocks = []
    for harmonic in range(1, H + 1):
        low = centre - centre // harmonic
        end = centre + (rows - 1 - centre) // harmonic + 1
        start = low // 16 * 16
        blocks.append((start, round_up(end, 16) - start))
    return blocks


def lane_gather(values, index):
    return jnp.take_along_axis(values, index, axis=1, mode="promise_in_bounds")


def pack_templates(templates, offsets):
    rows, parts, taps = templates.shape
    wide = jnp.broadcast_to(jnp.pad(offsets, (0, taps - rows)), (1, parts, taps))
    return jnp.concatenate([templates, wide.astype(templates.dtype)], axis=0)


def pick_margins(rows):
    centre = rows // 2
    reach = [
        (centre + harmonic * (start - centre), centre + harmonic * (start + count - 1 - centre))
        for harmonic, (start, count) in enumerate(row_blocks(rows), 1)
    ]
    return round_up(max(0, -min(low for low, _ in reach)), 8), round_up(max(0, max(high for _, high in reach) + 1 - rows), 8)


def pick_kernel(*refs, masks, shard_rows, rows):
    held = refs[: len(masks)]
    picked, taps = refs[len(masks) :]
    acc_index = lax.axis_index("acc")
    tap_tiles = held[0].shape[2] // LANES
    tiles = tap_tiles + 1
    before_rows, after_rows = pick_margins(rows)
    lane = lax.broadcasted_iota(jnp.int32, (shard_rows, LANES), 1)
    spot = lax.broadcasted_iota(jnp.int32, (shard_rows, shard_rows), 0) == lax.broadcasted_iota(
        jnp.int32, (shard_rows, shard_rows), 1
    )
    taps[:, :before_rows, :] = jnp.zeros((2 * tiles, before_rows, LANES), jnp.float32)
    taps[:, before_rows + rows :, :] = jnp.zeros((2 * tiles, taps.shape[1] - before_rows - rows, LANES), jnp.float32)
    for slot, mask in enumerate(masks):
        packed = held[slot][shard_rows, 0:1, :shard_rows].astype(jnp.float32)
        offset = jnp.sum(jnp.where(spot, packed, 0.0), axis=1, keepdims=True)
        offset = jnp.broadcast_to(offset.astype(jnp.int32), (shard_rows, LANES))
        index = (lane - offset) & (LANES - 1)
        stays = lane >= offset
        first_row = before_rows + (acc_index ^ mask) * shard_rows
        for part in range(2):
            values = held[slot][:shard_rows, part, :].astype(jnp.float32)
            before = jnp.zeros((shard_rows, LANES), jnp.float32)
            for tile in range(tiles):
                if tile < tap_tiles:
                    turned = lane_gather(values[:, tile * LANES : (tile + 1) * LANES], index)
                else:
                    turned = jnp.zeros((shard_rows, LANES), jnp.float32)
                taps[part * tiles + tile, pl.ds(first_row, shard_rows), :] = jnp.where(stays, turned, before)
                before = turned

    centre = rows // 2
    at = 0
    for harmonic, (start, count) in enumerate(row_blocks(rows), 1):
        first_row = before_rows + centre + harmonic * (start - centre)
        for part in range(2):
            for tile in range(tiles):
                chosen = taps[part * tiles + tile, pl.ds(first_row, count, stride=harmonic), :]
                picked[at : at + count, tile * LANES : (tile + 1) * LANES] = chosen.astype(jnp.bfloat16)
            at += count


def pick_templates(held, masks, rows):
    shard_rows = held[0].shape[0] - 1
    picked_rows = 2 * sum(count for _, count in row_blocks(rows))
    return pl.pallas_call(
        functools.partial(pick_kernel, masks=masks, shard_rows=shard_rows, rows=rows),
        out_shape=jax.ShapeDtypeStruct((picked_rows, WIDTH), jnp.bfloat16),
        in_specs=[VMEM] * len(masks),
        out_specs=VMEM,
        scratch_shapes=[pltpu.VMEM((2 * WIDTH // LANES, rows + sum(pick_margins(rows)), LANES), jnp.float32)],
        compiler_params=pltpu.CompilerParams(vmem_limit_bytes=16 << 20),
        name="pick_templates",
    )(*held)


def harmonic_kernel(*refs, n_slabs, rows):
    slabs = refs[:n_slabs]
    picked, out_ref, line, windows, total = refs[n_slabs:]
    sub_bins = out_ref.shape[1]
    blocks_f = sub_bins // LANES
    window_tiles = WIDTH // LANES
    slab_tiles = slabs[0].shape[1] // LANES
    filled = n_slabs * slab_tiles
    freq_index = lax.axis_index("freq")
    acc_index = lax.axis_index("acc")
    blocks = row_blocks(rows)

    line[:, filled:, :] = jnp.zeros((2, line.shape[1] - filled, LANES), jnp.float32)
    for mask, slab in zip(range(n_slabs - 1, -1, -1), slabs):
        values = slab[...].astype(jnp.float32)
        place = (freq_index ^ mask) * slab_tiles
        for tile in range(slab_tiles):
            for part in range(2):
                line[part, pl.ds(place + tile, 1), :] = values[part : part + 1, tile * LANES : (tile + 1) * LANES]

    lane = lax.broadcasted_iota(jnp.int32, (16, LANES), 1)
    sublane = lax.broadcasted_iota(jnp.int32, (16, LANES), 0)
    total[...] = jnp.zeros_like(total)
    at = 0
    for harmonic in range(1, H + 1):
        place = lane + harmonic * sublane
        index = place & (LANES - 1)
        stays = place < LANES
        n_tiles = window_tiles + harmonic * blocks_f
        first = jnp.minimum(harmonic * (freq_index * slab_tiles + acc_index * blocks_f), filled)
        for part in range(2):
            turned = []
            for tile in range(n_tiles + 1):
                values = jnp.broadcast_to(line[part, pl.ds(first + tile, 1), :], (16, LANES))
                turned.append(lane_gather(values, index))
            base = [jnp.where(stays, turned[t], turned[t + 1]).astype(jnp.bfloat16) for t in range(n_tiles)]
            moved = {0: base}
            for group in range(LANES // 16):
                tile_by, lane_by = divmod(16 * harmonic * group, LANES)
                if lane_by not in moved:
                    rolled = [pltpu.roll(values, LANES - lane_by, 1) for values in base]
                    keep = lane < LANES - lane_by
                    moved[lane_by] = [jnp.where(keep, rolled[t], rolled[min(t + 1, n_tiles - 1)]) for t in range(n_tiles)]
                for block in range(blocks_f):
                    for tile in range(window_tiles):
                        row = block * LANES + 16 * group
                        windows[harmonic - 1, part, row : row + 16, tile * LANES : (tile + 1) * LANES] = moved[lane_by][
                            tile_by + harmonic * block + tile
                        ]
        start, count = blocks[harmonic - 1]
        chosen = picked[at : at + 2 * count, :]
        at += 2 * count
        with_real = lax.dot_general(chosen, windows[harmonic - 1, 0], NT, preferred_element_type=jnp.float32)
        with_imag = lax.dot_general(chosen, windows[harmonic - 1, 1], NT, preferred_element_type=jnp.float32)
        real = with_real[:count] - with_imag[count:]
        imag = with_imag[:count] + with_real[count:]
        power = (real * real + imag * imag).astype(jnp.bfloat16)
        total[start : start + count, :] += power.astype(jnp.float32)
    out_ref[...] = total[:rows, :]


def harmonic_sums(slabs, picked, rows, sub_bins):
    filled = len(slabs) * slabs[0].shape[1] // LANES
    beyond = WIDTH // LANES + H * (sub_bins // LANES) + 1
    return pl.pallas_call(
        functools.partial(harmonic_kernel, n_slabs=len(slabs), rows=rows),
        out_shape=jax.ShapeDtypeStruct((rows, sub_bins), jnp.float32),
        in_specs=[VMEM] * (len(slabs) + 1),
        out_specs=VMEM,
        scratch_shapes=[
            pltpu.VMEM((2, filled + beyond, LANES), jnp.float32),
            pltpu.VMEM((H, 2, sub_bins, WIDTH), jnp.bfloat16),
            pltpu.VMEM((round_up(rows, 16), sub_bins), jnp.float32),
        ],
        compiler_params=pltpu.CompilerParams(vmem_limit_bytes=32 << 20),
        name="harmonic_sums",
    )(*slabs, picked)


def exchanged(value, axis):
    count = lax.axis_size(axis)
    masks = range(count - 1, 0, -1)
    return [lax.ppermute(value, axis, [(i, i ^ mask) for i in range(count)]) for mask in masks] + [value]


def shards(spectrum, templates, offsets):
    acc_count = lax.axis_size("acc")
    rows = acc_count * templates.shape[1]
    slabs = exchanged(spectrum, "freq")
    held = exchanged(pack_templates(jnp.transpose(templates, (1, 0, 2)), offsets), "acc")[::-1]
    picked = pick_templates(held, range(acc_count), rows)
    return harmonic_sums(slabs, picked, rows, spectrum.shape[1] // acc_count)


def solution(mesh):
    return jax.shard_map(
        shards,
        mesh=mesh,
        in_specs=(P(None, ("trial", "freq")), P(None, "acc", None), P("acc")),
        out_specs=P(None, ("trial", "freq", "acc")),
        check_vma=False,
    )
```

```python
import functools

import jax
import jax.numpy as jnp
from jax import lax
from jax.experimental import pallas as pl
from jax.experimental.pallas import tpu as pltpu
from jax.sharding import PartitionSpec as P

K = 384
OFF = 128
H = 8
LANES = 128
WIDTH = K + OFF
NT = (((1,), (1,)), ((), ()))
VMEM = pl.BlockSpec(memory_space=pltpu.VMEM)


def round_up(value, step):
    return (value + step - 1) // step * step


def row_blocks(rows):
    centre = rows // 2
    blocks = []
    for harmonic in range(1, H + 1):
        low = centre - centre // harmonic
        end = centre + (rows - 1 - centre) // harmonic + 1
        start = low // 16 * 16
        blocks.append((start, round_up(end, 16) - start))
    return blocks


def lane_gather(values, index):
    return jnp.take_along_axis(values, index, axis=1, mode="promise_in_bounds")


def pack_templates(templates, offsets):
    rows, parts, taps = templates.shape
    wide = jnp.broadcast_to(jnp.pad(offsets, (0, taps - rows)), (1, parts, taps))
    return jnp.concatenate([templates, wide.astype(templates.dtype)], axis=0)


def pick_margins(rows):
    centre = rows // 2
    reach = [
        (centre + harmonic * (start - centre), centre + harmonic * (start + count - 1 - centre))
        for harmonic, (start, count) in enumerate(row_blocks(rows), 1)
    ]
    return round_up(max(0, -min(low for low, _ in reach)), 8), round_up(max(0, max(high for _, high in reach) + 1 - rows), 8)


def place_templates(held, taps, masks, shard_rows, rows):
    acc_index = lax.axis_index("acc")
    tap_tiles = held[0].shape[2] // LANES
    tiles = tap_tiles + 1
    before_rows, after_rows = pick_margins(rows)
    lane = lax.broadcasted_iota(jnp.int32, (shard_rows, LANES), 1)
    spot = lax.broadcasted_iota(jnp.int32, (shard_rows, shard_rows), 0) == lax.broadcasted_iota(
        jnp.int32, (shard_rows, shard_rows), 1
    )
    taps[:, :before_rows, :] = jnp.zeros((2 * tiles, before_rows, LANES), jnp.float32)
    taps[:, before_rows + rows :, :] = jnp.zeros((2 * tiles, taps.shape[1] - before_rows - rows, LANES), jnp.float32)
    for slot, mask in enumerate(masks):
        packed = held[slot][shard_rows, 0:1, :shard_rows].astype(jnp.float32)
        offset = jnp.sum(jnp.where(spot, packed, 0.0), axis=1, keepdims=True)
        offset = jnp.broadcast_to(offset.astype(jnp.int32), (shard_rows, LANES))
        index = (lane - offset) & (LANES - 1)
        stays = lane >= offset
        first_row = before_rows + (acc_index ^ mask) * shard_rows
        for part in range(2):
            values = held[slot][:shard_rows, part, :].astype(jnp.float32)
            before = jnp.zeros((shard_rows, LANES), jnp.float32)
            for tile in range(tiles):
                if tile < tap_tiles:
                    turned = lane_gather(values[:, tile * LANES : (tile + 1) * LANES], index)
                else:
                    turned = jnp.zeros((shard_rows, LANES), jnp.float32)
                taps[part * tiles + tile, pl.ds(first_row, shard_rows), :] = jnp.where(stays, turned, before)
                before = turned


def windows_kernel(*refs):
    slabs = refs[:-2]
    windows, line = refs[-2:]
    sub_bins = windows.shape[2]
    blocks_f = sub_bins // LANES
    window_tiles = WIDTH // LANES
    slab_tiles = slabs[0].shape[1] // LANES
    filled = len(slabs) * slab_tiles
    freq_index = lax.axis_index("freq")
    acc_index = lax.axis_index("acc")

    line[:, filled:, :] = jnp.zeros((2, line.shape[1] - filled, LANES), jnp.float32)
    for mask, slab in zip(range(len(slabs) - 1, -1, -1), slabs):
        values = slab[...].astype(jnp.float32)
        place = (freq_index ^ mask) * slab_tiles
        for tile in range(slab_tiles):
            for part in range(2):
                line[part, pl.ds(place + tile, 1), :] = values[part : part + 1, tile * LANES : (tile + 1) * LANES]

    lane = lax.broadcasted_iota(jnp.int32, (16, LANES), 1)
    sublane = lax.broadcasted_iota(jnp.int32, (16, LANES), 0)
    for harmonic in range(1, H + 1):
        place = lane + harmonic * sublane
        index = place & (LANES - 1)
        stays = place < LANES
        n_tiles = window_tiles + harmonic * blocks_f
        first = jnp.minimum(harmonic * (freq_index * slab_tiles + acc_index * blocks_f), filled)
        for part in range(2):
            turned = []
            for tile in range(n_tiles + 1):
                values = jnp.broadcast_to(line[part, pl.ds(first + tile, 1), :], (16, LANES))
                turned.append(lane_gather(values, index))
            base = [jnp.where(stays, turned[t], turned[t + 1]) for t in range(n_tiles)]
            moved = {0: [values.astype(jnp.bfloat16) for values in base]}
            for group in range(LANES // 16):
                tile_by, lane_by = divmod(16 * harmonic * group, LANES)
                if lane_by not in moved:
                    rolled = [pltpu.roll(values, LANES - lane_by, 1) for values in base]
                    keep = lane < LANES - lane_by
                    moved[lane_by] = [
                        jnp.where(keep, rolled[t], rolled[min(t + 1, n_tiles - 1)]).astype(jnp.bfloat16)
                        for t in range(n_tiles)
                    ]
                for block in range(blocks_f):
                    for tile in range(window_tiles):
                        row = block * LANES + 16 * group
                        windows[harmonic - 1, part, row : row + 16, tile * LANES : (tile + 1) * LANES] = moved[lane_by][
                            tile_by + harmonic * block + tile
                        ]


def spectrum_windows(slabs, sub_bins):
    filled = len(slabs) * slabs[0].shape[1] // LANES
    beyond = WIDTH // LANES + H * (sub_bins // LANES) + 1
    return pl.pallas_call(
        windows_kernel,
        out_shape=jax.ShapeDtypeStruct((H, 2, sub_bins, WIDTH), jnp.bfloat16),
        in_specs=[VMEM] * len(slabs),
        out_specs=VMEM,
        scratch_shapes=[pltpu.VMEM((2, filled + beyond, LANES), jnp.float32)],
        compiler_params=pltpu.CompilerParams(vmem_limit_bytes=16 << 20),
        cost_estimate=pl.CostEstimate(flops=10**12, bytes_accessed=4000 << 20, transcendentals=0),
        name="spectrum_windows",
    )(*slabs)


def sums_kernel(*refs, masks, shard_rows, rows):
    windows = refs[0]
    held = refs[1 : len(masks) + 1]
    out_ref, taps, total = refs[len(masks) + 1 :]
    place_templates(held, taps, masks, shard_rows, rows)
    before_rows, _ = pick_margins(rows)
    tiles = WIDTH // LANES
    centre = rows // 2
    total[...] = jnp.zeros_like(total)
    for harmonic, (start, count) in enumerate(row_blocks(rows), 1):
        first_row = before_rows + centre + harmonic * (start - centre)
        chosen = jnp.concatenate(
            [
                jnp.concatenate(
                    [
                        taps[part * tiles + tile, pl.ds(first_row, count, stride=harmonic), :].astype(jnp.bfloat16)
                        for tile in range(tiles)
                    ],
                    axis=1,
                )
                for part in range(2)
            ],
            axis=0,
        )
        with_real = lax.dot_general(chosen, windows[harmonic - 1, 0], NT, preferred_element_type=jnp.float32)
        with_imag = lax.dot_general(chosen, windows[harmonic - 1, 1], NT, preferred_element_type=jnp.float32)
        real = with_real[:count] - with_imag[count:]
        imag = with_imag[:count] + with_real[count:]
        power = (real * real + imag * imag).astype(jnp.bfloat16)
        total[start : start + count, :] += power.astype(jnp.float32)
    out_ref[...] = total[:rows, :]


def harmonic_sums(windows, held, masks, rows):
    shard_rows = held[0].shape[0] - 1
    sub_bins = windows.shape[2]
    return pl.pallas_call(
        functools.partial(sums_kernel, masks=masks, shard_rows=shard_rows, rows=rows),
        out_shape=jax.ShapeDtypeStruct((rows, sub_bins), jnp.float32),
        in_specs=[VMEM] * (1 + len(masks)),
        out_specs=VMEM,
        scratch_shapes=[
            pltpu.VMEM((2 * WIDTH // LANES, rows + sum(pick_margins(rows)), LANES), jnp.float32),
            pltpu.VMEM((round_up(rows, 16), sub_bins), jnp.float32),
        ],
        compiler_params=pltpu.CompilerParams(vmem_limit_bytes=16 << 20),
        name="harmonic_sums",
    )(windows, *held)


def exchanged(value, axis):
    count = lax.axis_size(axis)
    masks = range(count - 1, 0, -1)
    return [lax.ppermute(value, axis, [(i, i ^ mask) for i in range(count)]) for mask in masks] + [value]


def shards(spectrum, templates, offsets):
    acc_count = lax.axis_size("acc")
    rows = acc_count * templates.shape[1]
    windows = spectrum_windows(exchanged(spectrum, "freq"), spectrum.shape[1] // acc_count)
    held = exchanged(pack_templates(jnp.transpose(templates, (1, 0, 2)), offsets), "acc")[::-1]
    return harmonic_sums(windows, held, range(acc_count), rows)


def solution(mesh):
    return jax.shard_map(
        shards,
        mesh=mesh,
        in_specs=(P(None, ("trial", "freq")), P(None, "acc", None), P("acc")),
        out_specs=P(None, ("trial", "freq", "acc")),
        check_vma=False,
    )
```

```python
import functools

import jax
import jax.numpy as jnp
from jax import lax
from jax.experimental import pallas as pl
from jax.experimental.pallas import tpu as pltpu
from jax.sharding import PartitionSpec as P

K = 384
OFF = 128
H = 8
LANES = 128
WIDTH = K + OFF
NT = (((1,), (1,)), ((), ()))
VMEM = pl.BlockSpec(memory_space=pltpu.VMEM)


def round_up(value, step):
    return (value + step - 1) // step * step


def row_blocks(rows):
    centre = rows // 2
    blocks = []
    for harmonic in range(1, H + 1):
        low = centre - centre // harmonic
        end = centre + (rows - 1 - centre) // harmonic + 1
        start = low // 16 * 16
        blocks.append((start, round_up(end, 16) - start))
    return blocks


def lane_gather(values, index):
    return jnp.take_along_axis(values, index, axis=1, mode="promise_in_bounds")


def pack_templates(templates, offsets):
    rows, parts, taps = templates.shape
    wide = jnp.broadcast_to(jnp.pad(offsets, (0, taps - rows)), (1, parts, taps))
    return jnp.concatenate([templates, wide.astype(templates.dtype)], axis=0)


def pick_margins(rows):
    centre = rows // 2
    reach = [
        (centre + harmonic * (start - centre), centre + harmonic * (start + count - 1 - centre))
        for harmonic, (start, count) in enumerate(row_blocks(rows), 1)
    ]
    return round_up(max(0, -min(low for low, _ in reach)), 8), round_up(max(0, max(high for _, high in reach) + 1 - rows), 8)


def pick_kernel(*refs, masks, shard_rows, rows):
    held = refs[: len(masks)]
    picked, taps = refs[len(masks) :]
    acc_index = lax.axis_index("acc")
    tap_tiles = held[0].shape[2] // LANES
    tiles = tap_tiles + 1
    before_rows, after_rows = pick_margins(rows)
    lane = lax.broadcasted_iota(jnp.int32, (shard_rows, LANES), 1)
    spot = lax.broadcasted_iota(jnp.int32, (shard_rows, shard_rows), 0) == lax.broadcasted_iota(
        jnp.int32, (shard_rows, shard_rows), 1
    )
    taps[:, :before_rows, :] = jnp.zeros((2 * tiles, before_rows, LANES), jnp.float32)
    taps[:, before_rows + rows :, :] = jnp.zeros((2 * tiles, taps.shape[1] - before_rows - rows, LANES), jnp.float32)
    for slot, mask in enumerate(masks):
        packed = held[slot][shard_rows, 0:1, :shard_rows].astype(jnp.float32)
        offset = jnp.sum(jnp.where(spot, packed, 0.0), axis=1, keepdims=True)
        offset = jnp.broadcast_to(offset.astype(jnp.int32), (shard_rows, LANES))
        index = (lane - offset) & (LANES - 1)
        stays = lane >= offset
        first_row = before_rows + (acc_index ^ mask) * shard_rows
        for part in range(2):
            values = held[slot][:shard_rows, part, :].astype(jnp.float32)
            before = jnp.zeros((shard_rows, LANES), jnp.float32)
            for tile in range(tiles):
                if tile < tap_tiles:
                    turned = lane_gather(values[:, tile * LANES : (tile + 1) * LANES], index)
                else:
                    turned = jnp.zeros((shard_rows, LANES), jnp.float32)
                taps[part * tiles + tile, pl.ds(first_row, shard_rows), :] = jnp.where(stays, turned, before)
                before = turned

    centre = rows // 2
    at = 0
    for harmonic, (start, count) in enumerate(row_blocks(rows), 1):
        first_row = before_rows + centre + harmonic * (start - centre)
        for part in range(2):
            for tile in range(tiles):
                chosen = taps[part * tiles + tile, pl.ds(first_row, count, stride=harmonic), :]
                picked[at : at + count, tile * LANES : (tile + 1) * LANES] = chosen.astype(jnp.bfloat16)
            at += count


def pick_templates(held, masks, rows):
    shard_rows = held[0].shape[0] - 1
    picked_rows = 2 * sum(count for _, count in row_blocks(rows))
    return pl.pallas_call(
        functools.partial(pick_kernel, masks=masks, shard_rows=shard_rows, rows=rows),
        out_shape=jax.ShapeDtypeStruct((picked_rows, WIDTH), jnp.bfloat16),
        in_specs=[VMEM] * len(masks),
        out_specs=VMEM,
        scratch_shapes=[pltpu.VMEM((2 * WIDTH // LANES, rows + sum(pick_margins(rows)), LANES), jnp.float32)],
        compiler_params=pltpu.CompilerParams(vmem_limit_bytes=16 << 20),
        name="pick_templates",
    )(*held)


def harmonic_kernel(*refs, n_slabs, rows):
    slabs = refs[:n_slabs]
    picked, out_ref, line, windows, total = refs[n_slabs:]
    sub_bins = out_ref.shape[1]
    blocks_f = sub_bins // LANES
    window_tiles = WIDTH // LANES
    slab_tiles = slabs[0].shape[1] // LANES
    filled = n_slabs * slab_tiles
    freq_index = lax.axis_index("freq")
    acc_index = lax.axis_index("acc")
    blocks = row_blocks(rows)

    line[:, filled:, :] = jnp.zeros((2, line.shape[1] - filled, LANES), jnp.float32)
    for (even, odd), slab in zip(slab_slots(n_slabs), slabs):
        values = slab[...].astype(jnp.float32)
        ahead = even + (odd - even) * (acc_index & 1)
        place = lax.rem(freq_index + ahead, n_slabs) * slab_tiles
        for tile in range(slab_tiles):
            for part in range(2):
                line[part, pl.ds(place + tile, 1), :] = values[part : part + 1, tile * LANES : (tile + 1) * LANES]

    lane = lax.broadcasted_iota(jnp.int32, (16, LANES), 1)
    sublane = lax.broadcasted_iota(jnp.int32, (16, LANES), 0)
    total[...] = jnp.zeros_like(total)
    at = [0]
    for _, count in blocks:
        at.append(at[-1] + 2 * count)

    def build(harmonic):
        place = lane + harmonic * sublane
        index = place & (LANES - 1)
        stays = place < LANES
        n_tiles = window_tiles + harmonic * blocks_f
        first = jnp.minimum(harmonic * (freq_index * slab_tiles + acc_index * blocks_f), filled)
        for part in range(2):
            turned = []
            for tile in range(n_tiles + 1):
                values = jnp.broadcast_to(line[part, pl.ds(first + tile, 1), :], (16, LANES))
                turned.append(lane_gather(values, index))
            base = [jnp.where(stays, turned[t], turned[t + 1]) for t in range(n_tiles)]
            moved = {0: [values.astype(jnp.bfloat16) for values in base]}
            for group in range(LANES // 16):
                tile_by, lane_by = divmod(16 * harmonic * group, LANES)
                if lane_by not in moved:
                    rolled = [pltpu.roll(values, LANES - lane_by, 1) for values in base]
                    keep = lane < LANES - lane_by
                    moved[lane_by] = [
                        jnp.where(keep, rolled[t], rolled[min(t + 1, n_tiles - 1)]).astype(jnp.bfloat16)
                        for t in range(n_tiles)
                    ]
                for block in range(blocks_f):
                    for tile in range(window_tiles):
                        row = block * LANES + 16 * group
                        windows[harmonic - 1, part, row : row + 16, tile * LANES : (tile + 1) * LANES] = moved[lane_by][
                            tile_by + harmonic * block + tile
                        ]

    def multiply(harmonic):
        start, count = blocks[harmonic - 1]
        chosen = picked[at[harmonic - 1] : at[harmonic], :]
        with_real = lax.dot_general(chosen, windows[harmonic - 1, 0], NT, preferred_element_type=jnp.float32)
        with_imag = lax.dot_general(chosen, windows[harmonic - 1, 1], NT, preferred_element_type=jnp.float32)
        real = with_real[:count] - with_imag[count:]
        imag = with_imag[:count] + with_real[count:]
        power = (real * real + imag * imag).astype(jnp.bfloat16)
        total[start : start + count, :] += power.astype(jnp.float32)

    for harmonic in range(1, H + 1):
        build(harmonic)
        multiply(harmonic)
    out_ref[...] = total[:rows, :]


def harmonic_sums(slabs, picked, rows, sub_bins):
    filled = len(slabs) * slabs[0].shape[1] // LANES
    beyond = WIDTH // LANES + H * (sub_bins // LANES) + 1
    return pl.pallas_call(
        functools.partial(harmonic_kernel, n_slabs=len(slabs), rows=rows),
        out_shape=jax.ShapeDtypeStruct((rows, sub_bins), jnp.float32),
        in_specs=[VMEM] * (len(slabs) + 1),
        out_specs=VMEM,
        scratch_shapes=[
            pltpu.VMEM((2, filled + beyond, LANES), jnp.float32),
            pltpu.VMEM((H, 2, sub_bins, WIDTH), jnp.bfloat16),
            pltpu.VMEM((round_up(rows, 16), sub_bins), jnp.float32),
        ],
        compiler_params=pltpu.CompilerParams(vmem_limit_bytes=32 << 20),
        name="harmonic_sums",
    )(*slabs, picked)


def slab_steps(freq_count):
    ahead = list(range(freq_count - 1, 0, -1))
    return [(ahead[i], ahead[min(i + 1, len(ahead) - 1)]) for i in range(0, len(ahead), 2)]


def slab_slots(freq_count):
    steps = slab_steps(freq_count)
    return steps + [(odd, even) for even, odd in steps if even != odd] + [(0, 0)]


def swapped(value, mask):
    return lax.ppermute(value, "acc", [(i, i ^ mask) for i in range(lax.axis_size("acc"))])


def gathered_slabs(spectrum):
    freq_count, acc_count = lax.axis_size("freq"), lax.axis_size("acc")
    fetched = []
    for step in slab_steps(freq_count):
        pairs = [
            ((i + step[a % 2]) % freq_count * acc_count + a, i * acc_count + a)
            for i in range(freq_count)
            for a in range(acc_count)
        ]
        fetched.append(lax.ppermute(spectrum, ("freq", "acc"), pairs))
    return fetched + [swapped(slab, 1) for slab, step in zip(fetched, slab_steps(freq_count)) if step[0] != step[1]] + [spectrum]


def gathered_templates(packed):
    return [packed] + [swapped(packed, mask) for mask in range(1, lax.axis_size("acc"))]


def shards(spectrum, templates, offsets):
    acc_count = lax.axis_size("acc")
    rows = acc_count * templates.shape[1]
    slabs = gathered_slabs(spectrum)
    held = gathered_templates(pack_templates(jnp.transpose(templates, (1, 0, 2)), offsets))
    picked = pick_templates(held, range(acc_count), rows)
    return harmonic_sums(slabs, picked, rows, spectrum.shape[1] // acc_count)


def solution(mesh):
    return jax.shard_map(
        shards,
        mesh=mesh,
        in_specs=(P(None, ("trial", "freq")), P(None, "acc", None), P("acc")),
        out_specs=P(None, ("trial", "freq", "acc")),
        check_vma=False,
    )
```

```python
import functools

import jax
import jax.numpy as jnp
from jax import lax
from jax.experimental import pallas as pl
from jax.experimental.pallas import tpu as pltpu
from jax.sharding import PartitionSpec as P

K = 384
OFF = 128
H = 8
LANES = 128
WIDTH = K + OFF
NT = (((1,), (1,)), ((), ()))
VMEM = pl.BlockSpec(memory_space=pltpu.VMEM)


def round_up(value, step):
    return (value + step - 1) // step * step


def row_blocks(rows):
    centre = rows // 2
    blocks = []
    for harmonic in range(1, H + 1):
        low = centre - centre // harmonic
        end = centre + (rows - 1 - centre) // harmonic + 1
        start = low // 16 * 16
        blocks.append((start, round_up(end, 16) - start))
    return blocks


def lane_gather(values, index):
    return jnp.take_along_axis(values, index, axis=1, mode="promise_in_bounds")


def pack_templates(templates, offsets):
    rows, parts, taps = templates.shape
    wide = jnp.broadcast_to(jnp.pad(offsets, (0, taps - rows)), (1, parts, taps))
    return jnp.concatenate([templates, wide.astype(templates.dtype)], axis=0)


def pick_margins(rows):
    centre = rows // 2
    reach = [
        (centre + harmonic * (start - centre), centre + harmonic * (start + count - 1 - centre))
        for harmonic, (start, count) in enumerate(row_blocks(rows), 1)
    ]
    return round_up(max(0, -min(low for low, _ in reach)), 8), round_up(max(0, max(high for _, high in reach) + 1 - rows), 8)


def shift_kernel(packed_ref, out_ref):
    shard_rows = out_ref.shape[1]
    shift_rows(packed_ref, out_ref, pl.ds(0, shard_rows), shard_rows)


def shift_rows(packed_ref, out_ref, place, shard_rows):
    tap_tiles = packed_ref.shape[2] // LANES
    tiles = tap_tiles + 1
    lane = lax.broadcasted_iota(jnp.int32, (shard_rows, LANES), 1)
    spot = lax.broadcasted_iota(jnp.int32, (shard_rows, shard_rows), 0) == lax.broadcasted_iota(
        jnp.int32, (shard_rows, shard_rows), 1
    )
    packed = packed_ref[shard_rows, 0:1, :shard_rows].astype(jnp.float32)
    offset = jnp.sum(jnp.where(spot, packed, 0.0), axis=1, keepdims=True)
    offset = jnp.broadcast_to(offset.astype(jnp.int32), (shard_rows, LANES))
    index = (lane - offset) & (LANES - 1)
    stays = lane >= offset
    for part in range(2):
        values = packed_ref[:shard_rows, part, :].astype(jnp.float32)
        before = jnp.zeros((shard_rows, LANES), jnp.float32)
        for tile in range(tiles):
            if tile < tap_tiles:
                turned = lane_gather(values[:, tile * LANES : (tile + 1) * LANES], index)
            else:
                turned = jnp.zeros((shard_rows, LANES), jnp.float32)
            out_ref[part * tiles + tile, place, :] = jnp.where(stays, turned, before)
            before = turned


def shift_own(packed):
    shard_rows = packed.shape[0] - 1
    return pl.pallas_call(
        shift_kernel,
        out_shape=jax.ShapeDtypeStruct((2 * WIDTH // LANES, shard_rows, LANES), jnp.float32),
        in_specs=[VMEM],
        out_specs=VMEM,
        compiler_params=pltpu.CompilerParams(vmem_limit_bytes=4 << 20),
        cost_estimate=pl.CostEstimate(flops=2 * 10**9, bytes_accessed=1 << 20, transcendentals=0),
        name="shift_own",
    )(packed)


def pick_kernel(*refs, masks, shard_rows, rows):
    held = refs[: len(masks)]
    picked, taps = refs[len(masks) :]
    acc_index = lax.axis_index("acc")
    tiles = WIDTH // LANES
    before_rows, after_rows = pick_margins(rows)
    taps[:, :before_rows, :] = jnp.zeros((2 * tiles, before_rows, LANES), jnp.float32)
    taps[:, before_rows + rows :, :] = jnp.zeros((2 * tiles, taps.shape[1] - before_rows - rows, LANES), jnp.float32)
    for slot, mask in enumerate(masks):
        place = pl.ds(before_rows + (acc_index ^ mask) * shard_rows, shard_rows)
        if slot == 0:
            for tile in range(2 * tiles):
                taps[tile, place, :] = held[0][tile]
        else:
            shift_rows(held[slot], taps, place, shard_rows)

    centre = rows // 2
    at = 0
    for harmonic, (start, count) in enumerate(row_blocks(rows), 1):
        first_row = before_rows + centre + harmonic * (start - centre)
        for part in range(2):
            for tile in range(tiles):
                chosen = taps[part * tiles + tile, pl.ds(first_row, count, stride=harmonic), :]
                picked[at : at + count, tile * LANES : (tile + 1) * LANES] = chosen.astype(jnp.bfloat16)
            at += count


def pick_templates(held, masks, rows):
    shard_rows = held[0].shape[1]
    picked_rows = 2 * sum(count for _, count in row_blocks(rows))
    return pl.pallas_call(
        functools.partial(pick_kernel, masks=masks, shard_rows=shard_rows, rows=rows),
        out_shape=jax.ShapeDtypeStruct((picked_rows, WIDTH), jnp.bfloat16),
        in_specs=[VMEM] * len(masks),
        out_specs=VMEM,
        scratch_shapes=[pltpu.VMEM((2 * WIDTH // LANES, rows + sum(pick_margins(rows)), LANES), jnp.float32)],
        compiler_params=pltpu.CompilerParams(vmem_limit_bytes=16 << 20),
        name="pick_templates",
    )(*held)


def harmonic_kernel(*refs, n_slabs, rows):
    slabs = refs[:n_slabs]
    picked, out_ref, line, windows, total = refs[n_slabs:]
    sub_bins = out_ref.shape[1]
    blocks_f = sub_bins // LANES
    window_tiles = WIDTH // LANES
    slab_tiles = slabs[0].shape[1] // LANES
    filled = n_slabs * slab_tiles
    freq_index = lax.axis_index("freq")
    acc_index = lax.axis_index("acc")
    blocks = row_blocks(rows)

    line[:, filled:, :] = jnp.zeros((2, line.shape[1] - filled, LANES), jnp.float32)
    for (even, odd), slab in zip(slab_slots(n_slabs), slabs):
        values = slab[...].astype(jnp.float32)
        ahead = even + (odd - even) * (acc_index & 1)
        place = lax.rem(freq_index + ahead, n_slabs) * slab_tiles
        for tile in range(slab_tiles):
            for part in range(2):
                line[part, pl.ds(place + tile, 1), :] = values[part : part + 1, tile * LANES : (tile + 1) * LANES]

    lane = lax.broadcasted_iota(jnp.int32, (16, LANES), 1)
    sublane = lax.broadcasted_iota(jnp.int32, (16, LANES), 0)
    total[...] = jnp.zeros_like(total)
    at = [0]
    for _, count in blocks:
        at.append(at[-1] + 2 * count)

    def build(harmonic):
        place = lane + harmonic * sublane
        index = place & (LANES - 1)
        stays = place < LANES
        n_tiles = window_tiles + harmonic * blocks_f
        first = jnp.minimum(harmonic * (freq_index * slab_tiles + acc_index * blocks_f), filled)
        for part in range(2):
            turned = []
            for tile in range(n_tiles + 1):
                values = jnp.broadcast_to(line[part, pl.ds(first + tile, 1), :], (16, LANES))
                turned.append(lane_gather(values, index))
            base = [jnp.where(stays, turned[t], turned[t + 1]) for t in range(n_tiles)]
            moved = {0: [values.astype(jnp.bfloat16) for values in base]}
            for group in range(LANES // 16):
                tile_by, lane_by = divmod(16 * harmonic * group, LANES)
                if lane_by not in moved:
                    rolled = [pltpu.roll(values, LANES - lane_by, 1) for values in base]
                    keep = lane < LANES - lane_by
                    moved[lane_by] = [
                        jnp.where(keep, rolled[t], rolled[min(t + 1, n_tiles - 1)]).astype(jnp.bfloat16)
                        for t in range(n_tiles)
                    ]
                for block in range(blocks_f):
                    for tile in range(window_tiles):
                        row = block * LANES + 16 * group
                        windows[harmonic - 1, part, row : row + 16, tile * LANES : (tile + 1) * LANES] = moved[lane_by][
                            tile_by + harmonic * block + tile
                        ]

    def multiply(harmonic):
        start, count = blocks[harmonic - 1]
        chosen = picked[at[harmonic - 1] : at[harmonic], :]
        with_real = lax.dot_general(chosen, windows[harmonic - 1, 0], NT, preferred_element_type=jnp.float32)
        with_imag = lax.dot_general(chosen, windows[harmonic - 1, 1], NT, preferred_element_type=jnp.float32)
        real = with_real[:count] - with_imag[count:]
        imag = with_imag[:count] + with_real[count:]
        power = (real * real + imag * imag).astype(jnp.bfloat16)
        total[start : start + count, :] += power.astype(jnp.float32)

    for harmonic in range(1, H + 1):
        build(harmonic)
        multiply(harmonic)
    out_ref[...] = total[:rows, :]


def harmonic_sums(slabs, picked, rows, sub_bins):
    filled = len(slabs) * slabs[0].shape[1] // LANES
    beyond = WIDTH // LANES + H * (sub_bins // LANES) + 1
    return pl.pallas_call(
        functools.partial(harmonic_kernel, n_slabs=len(slabs), rows=rows),
        out_shape=jax.ShapeDtypeStruct((rows, sub_bins), jnp.float32),
        in_specs=[VMEM] * (len(slabs) + 1),
        out_specs=VMEM,
        scratch_shapes=[
            pltpu.VMEM((2, filled + beyond, LANES), jnp.float32),
            pltpu.VMEM((H, 2, sub_bins, WIDTH), jnp.bfloat16),
            pltpu.VMEM((round_up(rows, 16), sub_bins), jnp.float32),
        ],
        compiler_params=pltpu.CompilerParams(vmem_limit_bytes=32 << 20),
        name="harmonic_sums",
    )(*slabs, picked)


def slab_steps(freq_count):
    ahead = list(range(freq_count - 1, 0, -1))
    return [(ahead[i], ahead[min(i + 1, len(ahead) - 1)]) for i in range(0, len(ahead), 2)]


def slab_slots(freq_count):
    steps = slab_steps(freq_count)
    return steps + [(odd, even) for even, odd in steps if even != odd] + [(0, 0)]


def swapped(value, mask):
    return lax.ppermute(value, "acc", [(i, i ^ mask) for i in range(lax.axis_size("acc"))])


def gathered_slabs(spectrum):
    freq_count, acc_count = lax.axis_size("freq"), lax.axis_size("acc")
    fetched = []
    for step in slab_steps(freq_count):
        pairs = [
            ((i + step[a % 2]) % freq_count * acc_count + a, i * acc_count + a)
            for i in range(freq_count)
            for a in range(acc_count)
            if i + step[a % 2] < freq_count
        ]
        fetched.append(lax.ppermute(spectrum, ("freq", "acc"), pairs))
    return fetched + [swapped(slab, 1) for slab, step in zip(fetched, slab_steps(freq_count)) if step[0] != step[1]] + [spectrum]


def gathered_templates(packed):
    return [shift_own(packed)] + [swapped(packed, mask) for mask in range(1, lax.axis_size("acc"))]


def shards(spectrum, templates, offsets):
    acc_count = lax.axis_size("acc")
    rows = acc_count * templates.shape[1]
    slabs = gathered_slabs(spectrum)
    held = gathered_templates(pack_templates(jnp.transpose(templates, (1, 0, 2)), offsets))
    picked = pick_templates(held, range(acc_count), rows)
    return harmonic_sums(slabs, picked, rows, spectrum.shape[1] // acc_count)


def solution(mesh):
    return jax.shard_map(
        shards,
        mesh=mesh,
        in_specs=(P(None, ("trial", "freq")), P(None, "acc", None), P("acc")),
        out_specs=P(None, ("trial", "freq", "acc")),
        check_vma=False,
    )
```

```python
import functools

import jax
import jax.numpy as jnp
from jax import lax
from jax.experimental import pallas as pl
from jax.experimental.pallas import tpu as pltpu
from jax.sharding import PartitionSpec as P

K = 384
OFF = 128
H = 8
LANES = 128
WIDTH = K + OFF
NT = (((1,), (1,)), ((), ()))
VMEM = pl.BlockSpec(memory_space=pltpu.VMEM)


def round_up(value, step):
    return (value + step - 1) // step * step


def row_blocks(rows):
    centre = rows // 2
    blocks = []
    for harmonic in range(1, H + 1):
        low = centre - centre // harmonic
        end = centre + (rows - 1 - centre) // harmonic + 1
        start = low // 16 * 16
        blocks.append((start, round_up(end, 16) - start))
    return blocks


def lane_gather(values, index):
    return jnp.take_along_axis(values, index, axis=1, mode="promise_in_bounds")


def pack_templates(templates, offsets):
    rows, parts, taps = templates.shape
    wide = jnp.broadcast_to(jnp.pad(offsets, (0, taps - rows)), (1, parts, taps))
    return jnp.concatenate([templates, wide.astype(templates.dtype)], axis=0)


def pick_margins(rows):
    centre = rows // 2
    reach = [
        (centre + harmonic * (start - centre), centre + harmonic * (start + count - 1 - centre))
        for harmonic, (start, count) in enumerate(row_blocks(rows), 1)
    ]
    return round_up(max(0, -min(low for low, _ in reach)), 8), round_up(max(0, max(high for _, high in reach) + 1 - rows), 8)


def shift_kernel(packed_ref, out_ref):
    shard_rows = out_ref.shape[1]
    shift_rows(packed_ref, out_ref, pl.ds(0, shard_rows), shard_rows)


def shift_rows(packed_ref, out_ref, place, shard_rows):
    tap_tiles = packed_ref.shape[2] // LANES
    tiles = tap_tiles + 1
    lane = lax.broadcasted_iota(jnp.int32, (shard_rows, LANES), 1)
    spot = lax.broadcasted_iota(jnp.int32, (shard_rows, shard_rows), 0) == lax.broadcasted_iota(
        jnp.int32, (shard_rows, shard_rows), 1
    )
    packed = packed_ref[shard_rows, 0:1, :shard_rows].astype(jnp.float32)
    offset = jnp.sum(jnp.where(spot, packed, 0.0), axis=1, keepdims=True)
    offset = jnp.broadcast_to(offset.astype(jnp.int32), (shard_rows, LANES))
    index = (lane - offset) & (LANES - 1)
    stays = lane >= offset
    for part in range(2):
        values = packed_ref[:shard_rows, part, :].astype(jnp.float32)
        before = jnp.zeros((shard_rows, LANES), jnp.float32)
        for tile in range(tiles):
            if tile < tap_tiles:
                turned = lane_gather(values[:, tile * LANES : (tile + 1) * LANES], index)
            else:
                turned = jnp.zeros((shard_rows, LANES), jnp.float32)
            out_ref[part * tiles + tile, place, :] = jnp.where(stays, turned, before)
            before = turned


def shift_own(packed):
    shard_rows = packed.shape[0] - 1
    return pl.pallas_call(
        shift_kernel,
        out_shape=jax.ShapeDtypeStruct((2 * WIDTH // LANES, shard_rows, LANES), jnp.float32),
        in_specs=[VMEM],
        out_specs=VMEM,
        compiler_params=pltpu.CompilerParams(vmem_limit_bytes=4 << 20),
        cost_estimate=pl.CostEstimate(flops=2 * 10**9, bytes_accessed=1 << 20, transcendentals=0),
        name="shift_own",
    )(packed)


def pick_kernel(*refs, masks, shard_rows, rows):
    held = refs[: len(masks)]
    picked, taps = refs[len(masks) :]
    acc_index = lax.axis_index("acc")
    tiles = WIDTH // LANES
    before_rows, after_rows = pick_margins(rows)
    taps[:, :before_rows, :] = jnp.zeros((2 * tiles, before_rows, LANES), jnp.float32)
    taps[:, before_rows + rows :, :] = jnp.zeros((2 * tiles, taps.shape[1] - before_rows - rows, LANES), jnp.float32)
    for slot, mask in enumerate(masks):
        place = pl.ds(before_rows + (acc_index ^ mask) * shard_rows, shard_rows)
        if slot == 0:
            for tile in range(2 * tiles):
                taps[tile, place, :] = held[0][tile]
        else:
            shift_rows(held[slot], taps, place, shard_rows)

    centre = rows // 2
    at = 0
    for harmonic, (start, count) in enumerate(row_blocks(rows), 1):
        first_row = before_rows + centre + harmonic * (start - centre)
        for part in range(2):
            for tile in range(tiles):
                chosen = taps[part * tiles + tile, pl.ds(first_row, count, stride=harmonic), :]
                picked[at : at + count, tile * LANES : (tile + 1) * LANES] = chosen.astype(jnp.bfloat16)
            at += count


def pick_templates(held, masks, rows):
    shard_rows = held[0].shape[1]
    picked_rows = 2 * sum(count for _, count in row_blocks(rows))
    return pl.pallas_call(
        functools.partial(pick_kernel, masks=masks, shard_rows=shard_rows, rows=rows),
        out_shape=jax.ShapeDtypeStruct((picked_rows, WIDTH), jnp.bfloat16),
        in_specs=[VMEM] * len(masks),
        out_specs=VMEM,
        scratch_shapes=[pltpu.VMEM((2 * WIDTH // LANES, rows + sum(pick_margins(rows)), LANES), jnp.float32)],
        compiler_params=pltpu.CompilerParams(vmem_limit_bytes=16 << 20),
        name="pick_templates",
    )(*held)


def harmonic_kernel(*refs, n_slabs, rows):
    slabs = refs[:n_slabs]
    picked, out_ref, line, windows, total = refs[n_slabs:]
    sub_bins = out_ref.shape[1]
    blocks_f = sub_bins // LANES
    window_tiles = WIDTH // LANES
    slab_tiles = slabs[0].shape[1] // LANES
    filled = n_slabs * slab_tiles
    freq_index = lax.axis_index("freq")
    acc_index = lax.axis_index("acc")
    blocks = row_blocks(rows)

    line[:, filled:, :] = jnp.zeros((2, line.shape[1] - filled, LANES), jnp.float32)
    for (even, odd), slab in zip(slab_slots(n_slabs), slabs):
        values = slab[...].astype(jnp.float32)
        ahead = even + (odd - even) * (acc_index & 1)
        place = lax.rem(freq_index + ahead, n_slabs) * slab_tiles
        for tile in range(slab_tiles):
            for part in range(2):
                line[part, pl.ds(place + tile, 1), :] = values[part : part + 1, tile * LANES : (tile + 1) * LANES]

    lane = lax.broadcasted_iota(jnp.int32, (16, LANES), 1)
    sublane = lax.broadcasted_iota(jnp.int32, (16, LANES), 0)
    total[...] = jnp.zeros_like(total)
    at = [0]
    for _, count in blocks:
        at.append(at[-1] + 2 * count)

    def build(harmonic):
        place = lane + harmonic * sublane
        index = place & (LANES - 1)
        stays = place < LANES
        n_tiles = window_tiles + harmonic * blocks_f
        first = jnp.minimum(harmonic * (freq_index * slab_tiles + acc_index * blocks_f), filled)
        for part in range(2):
            turned = []
            for tile in range(n_tiles + 1):
                values = jnp.broadcast_to(line[part, pl.ds(first + tile, 1), :], (16, LANES))
                turned.append(lane_gather(values, index))
            base = [jnp.where(stays, turned[t], turned[t + 1]) for t in range(n_tiles)]
            moved = {0: [values.astype(jnp.bfloat16) for values in base]}
            for group in range(LANES // 16):
                tile_by, lane_by = divmod(16 * harmonic * group, LANES)
                if lane_by not in moved:
                    rolled = [pltpu.roll(values, LANES - lane_by, 1) for values in base]
                    keep = lane < LANES - lane_by
                    moved[lane_by] = [
                        jnp.where(keep, rolled[t], rolled[min(t + 1, n_tiles - 1)]).astype(jnp.bfloat16)
                        for t in range(n_tiles)
                    ]
                for block in range(blocks_f):
                    for tile in range(window_tiles):
                        row = block * LANES + 16 * group
                        windows[harmonic - 1, part, row : row + 16, tile * LANES : (tile + 1) * LANES] = moved[lane_by][
                            tile_by + harmonic * block + tile
                        ]

    def multiply(harmonic):
        start, count = blocks[harmonic - 1]
        chosen = picked[at[harmonic - 1] : at[harmonic], :]
        with_real = lax.dot_general(chosen, windows[harmonic - 1, 0], NT, preferred_element_type=jnp.float32)
        with_imag = lax.dot_general(chosen, windows[harmonic - 1, 1], NT, preferred_element_type=jnp.float32)
        real = with_real[:count] - with_imag[count:]
        imag = with_imag[:count] + with_real[count:]
        power = (real * real + imag * imag).astype(jnp.bfloat16)
        total[start : start + count, :] += power.astype(jnp.float32)

    for harmonic in range(1, H + 1):
        build(harmonic)
        multiply(harmonic)
    out_ref[...] = total[:rows, :]


def harmonic_sums(slabs, picked, rows, sub_bins):
    filled = len(slabs) * slabs[0].shape[1] // LANES
    beyond = WIDTH // LANES + H * (sub_bins // LANES) + 1
    return pl.pallas_call(
        functools.partial(harmonic_kernel, n_slabs=len(slabs), rows=rows),
        out_shape=jax.ShapeDtypeStruct((rows, sub_bins), jnp.float32),
        in_specs=[VMEM] * (len(slabs) + 1),
        out_specs=VMEM,
        scratch_shapes=[
            pltpu.VMEM((2, filled + beyond, LANES), jnp.float32),
            pltpu.VMEM((H, 2, sub_bins, WIDTH), jnp.bfloat16),
            pltpu.VMEM((round_up(rows, 16), sub_bins), jnp.float32),
        ],
        compiler_params=pltpu.CompilerParams(vmem_limit_bytes=32 << 20),
        name="harmonic_sums",
    )(*slabs, picked)


def slab_steps(freq_count):
    ahead = list(range(freq_count - 1, 0, -1))
    return [(ahead[i], ahead[min(i + 1, len(ahead) - 1)]) for i in range(0, len(ahead), 2)]


def slab_slots(freq_count):
    steps = slab_steps(freq_count)
    return steps + [(odd, even) for even, odd in steps if even != odd] + [(0, 0)]


def swapped(value, mask):
    return lax.ppermute(value, "acc", [(i, i ^ mask) for i in range(lax.axis_size("acc"))])


def gathered_slabs(spectrum):
    freq_count, acc_count = lax.axis_size("freq"), lax.axis_size("acc")
    fetched = []
    for step in slab_steps(freq_count):
        pairs = [
            ((i + step[a % 2]) % freq_count * acc_count + a, i * acc_count + a)
            for i in range(freq_count)
            for a in range(acc_count)
            if i + step[a % 2] < freq_count
        ]
        fetched.append(lax.ppermute(spectrum, ("freq", "acc"), pairs))
    return fetched + [swapped(slab, 1) for slab, step in zip(fetched, slab_steps(freq_count)) if step[0] != step[1]] + [spectrum]


def gathered_templates(packed):
    return [shift_own(packed)] + [swapped(packed, mask) for mask in range(lax.axis_size("acc") - 1, 0, -1)]


def shards(spectrum, templates, offsets):
    acc_count = lax.axis_size("acc")
    rows = acc_count * templates.shape[1]
    slabs = gathered_slabs(spectrum)
    held = gathered_templates(pack_templates(jnp.transpose(templates, (1, 0, 2)), offsets))
    picked = pick_templates(held, [0, *range(acc_count - 1, 0, -1)], rows)
    return harmonic_sums(slabs, picked, rows, spectrum.shape[1] // acc_count)


def solution(mesh):
    return jax.shard_map(
        shards,
        mesh=mesh,
        in_specs=(P(None, ("trial", "freq")), P(None, "acc", None), P("acc")),
        out_specs=P(None, ("trial", "freq", "acc")),
        check_vma=False,
    )
```

```python
import functools

import jax
import jax.numpy as jnp
from jax import lax
from jax.experimental import pallas as pl
from jax.experimental.pallas import tpu as pltpu
from jax.sharding import PartitionSpec as P

K = 384
OFF = 128
H = 8
LANES = 128
WIDTH = K + OFF
NT = (((1,), (1,)), ((), ()))
VMEM = pl.BlockSpec(memory_space=pltpu.VMEM)


def round_up(value, step):
    return (value + step - 1) // step * step


def row_blocks(rows):
    centre = rows // 2
    blocks = []
    for harmonic in range(1, H + 1):
        low = centre - centre // harmonic
        end = centre + (rows - 1 - centre) // harmonic + 1
        start = low // 16 * 16
        blocks.append((start, round_up(end, 16) - start))
    return blocks


def lane_gather(values, index):
    return jnp.take_along_axis(values, index, axis=1, mode="promise_in_bounds")


def pack_templates(templates, offsets):
    rows, parts, taps = templates.shape
    wide = jnp.broadcast_to(jnp.pad(offsets, (0, taps - rows)), (1, parts, taps))
    return jnp.concatenate([templates, wide.astype(templates.dtype)], axis=0)


def pick_margins(rows):
    centre = rows // 2
    reach = [
        (centre + harmonic * (start - centre), centre + harmonic * (start + count - 1 - centre))
        for harmonic, (start, count) in enumerate(row_blocks(rows), 1)
    ]
    return round_up(max(0, -min(low for low, _ in reach)), 8), round_up(max(0, max(high for _, high in reach) + 1 - rows), 8)


def shift_kernel(packed_ref, out_ref):
    shard_rows = out_ref.shape[1]
    shift_rows(packed_ref, out_ref, pl.ds(0, shard_rows), shard_rows)


def shift_rows(packed_ref, out_ref, place, shard_rows):
    tap_tiles = packed_ref.shape[2] // LANES
    tiles = tap_tiles + 1
    lane = lax.broadcasted_iota(jnp.int32, (shard_rows, LANES), 1)
    spot = lax.broadcasted_iota(jnp.int32, (shard_rows, shard_rows), 0) == lax.broadcasted_iota(
        jnp.int32, (shard_rows, shard_rows), 1
    )
    packed = packed_ref[shard_rows, 0:1, :shard_rows].astype(jnp.float32)
    offset = jnp.sum(jnp.where(spot, packed, 0.0), axis=1, keepdims=True)
    offset = jnp.broadcast_to(offset.astype(jnp.int32), (shard_rows, LANES))
    index = (lane - offset) & (LANES - 1)
    stays = lane >= offset
    for part in range(2):
        values = packed_ref[:shard_rows, part, :].astype(jnp.float32)
        before = jnp.zeros((shard_rows, LANES), jnp.float32)
        for tile in range(tiles):
            if tile < tap_tiles:
                turned = lane_gather(values[:, tile * LANES : (tile + 1) * LANES], index)
            else:
                turned = jnp.zeros((shard_rows, LANES), jnp.float32)
            out_ref[part * tiles + tile, place, :] = jnp.where(stays, turned, before)
            before = turned


def shift_own(packed):
    shard_rows = packed.shape[0] - 1
    return pl.pallas_call(
        shift_kernel,
        out_shape=jax.ShapeDtypeStruct((2 * WIDTH // LANES, shard_rows, LANES), jnp.float32),
        in_specs=[VMEM],
        out_specs=VMEM,
        compiler_params=pltpu.CompilerParams(vmem_limit_bytes=4 << 20),
        cost_estimate=pl.CostEstimate(flops=2 * 10**9, bytes_accessed=1 << 20, transcendentals=0),
        name="shift_own",
    )(packed)


def pick_kernel(*refs, masks, shard_rows, rows):
    held = refs[: len(masks)]
    picked, taps = refs[len(masks) :]
    acc_index = lax.axis_index("acc")
    tiles = WIDTH // LANES
    before_rows, after_rows = pick_margins(rows)
    taps[:, :before_rows, :] = jnp.zeros((2 * tiles, before_rows, LANES), jnp.float32)
    taps[:, before_rows + rows :, :] = jnp.zeros((2 * tiles, taps.shape[1] - before_rows - rows, LANES), jnp.float32)
    for slot, mask in enumerate(masks):
        place = pl.ds(before_rows + (acc_index ^ mask) * shard_rows, shard_rows)
        if slot == 0:
            for tile in range(2 * tiles):
                taps[tile, place, :] = held[0][tile]
        else:
            shift_rows(held[slot], taps, place, shard_rows)

    centre = rows // 2
    at = 0
    for harmonic, (start, count) in enumerate(row_blocks(rows), 1):
        first_row = before_rows + centre + harmonic * (start - centre)
        for part in range(2):
            for tile in range(tiles):
                chosen = taps[part * tiles + tile, pl.ds(first_row, count, stride=harmonic), :]
                picked[at : at + count, tile * LANES : (tile + 1) * LANES] = chosen.astype(jnp.bfloat16)
            at += count


def pick_templates(held, masks, rows):
    shard_rows = held[0].shape[1]
    picked_rows = 2 * sum(count for _, count in row_blocks(rows))
    return pl.pallas_call(
        functools.partial(pick_kernel, masks=masks, shard_rows=shard_rows, rows=rows),
        out_shape=jax.ShapeDtypeStruct((picked_rows, WIDTH), jnp.bfloat16),
        in_specs=[VMEM] * len(masks),
        out_specs=VMEM,
        scratch_shapes=[pltpu.VMEM((2 * WIDTH // LANES, rows + sum(pick_margins(rows)), LANES), jnp.float32)],
        compiler_params=pltpu.CompilerParams(vmem_limit_bytes=16 << 20),
        name="pick_templates",
    )(*held)


def harmonic_kernel(*refs, n_slabs, rows):
    slabs = refs[:n_slabs]
    picked, out_ref, line, windows, total = refs[n_slabs:]
    sub_bins = out_ref.shape[1]
    blocks_f = sub_bins // LANES
    window_tiles = WIDTH // LANES
    slab_tiles = slabs[0].shape[1] // LANES
    filled = n_slabs * slab_tiles
    freq_index = lax.axis_index("freq")
    acc_index = lax.axis_index("acc")
    blocks = row_blocks(rows)

    line[:, filled:, :] = jnp.zeros((2, line.shape[1] - filled, LANES), jnp.float32)
    for (even, odd), slab in zip(slab_slots(n_slabs), slabs):
        values = slab[...].astype(jnp.float32)
        ahead = even + (odd - even) * (acc_index & 1)
        place = lax.rem(freq_index + ahead, n_slabs) * slab_tiles
        for tile in range(slab_tiles):
            for part in range(2):
                line[part, pl.ds(place + tile, 1), :] = values[part : part + 1, tile * LANES : (tile + 1) * LANES]

    lane = lax.broadcasted_iota(jnp.int32, (16, LANES), 1)
    sublane = lax.broadcasted_iota(jnp.int32, (16, LANES), 0)
    at = [0]
    for _, count in blocks:
        at.append(at[-1] + 2 * count)

    def build(harmonic):
        place = lane + harmonic * sublane
        index = place & (LANES - 1)
        stays = place < LANES
        n_tiles = window_tiles + harmonic * blocks_f
        first = jnp.minimum(harmonic * (freq_index * slab_tiles + acc_index * blocks_f), filled)
        for part in range(2):
            turned = []
            for tile in range(n_tiles + 1):
                values = jnp.broadcast_to(line[part, pl.ds(first + tile, 1), :], (16, LANES))
                turned.append(lane_gather(values, index))
            base = [jnp.where(stays, turned[t], turned[t + 1]) for t in range(n_tiles)]
            moved = {0: [values.astype(jnp.bfloat16) for values in base]}
            for group in range(LANES // 16):
                tile_by, lane_by = divmod(16 * harmonic * group, LANES)
                if lane_by not in moved:
                    rolled = [pltpu.roll(values, LANES - lane_by, 1) for values in base]
                    keep = lane < LANES - lane_by
                    moved[lane_by] = [
                        jnp.where(keep, rolled[t], rolled[min(t + 1, n_tiles - 1)]).astype(jnp.bfloat16)
                        for t in range(n_tiles)
                    ]
                for block in range(blocks_f):
                    for tile in range(window_tiles):
                        row = block * LANES + 16 * group
                        windows[harmonic - 1, part, row : row + 16, tile * LANES : (tile + 1) * LANES] = moved[lane_by][
                            tile_by + harmonic * block + tile
                        ]

    def multiply(harmonic):
        start, count = blocks[harmonic - 1]
        chosen = picked[at[harmonic - 1] : at[harmonic], :]
        with_real = lax.dot_general(chosen, windows[harmonic - 1, 0], NT, preferred_element_type=jnp.float32)
        with_imag = lax.dot_general(chosen, windows[harmonic - 1, 1], NT, preferred_element_type=jnp.float32)
        real = with_real[:count] - with_imag[count:]
        imag = with_imag[:count] + with_real[count:]
        power = (real * real + imag * imag).astype(jnp.bfloat16)
        if harmonic == 1:
            total[...] = power.astype(jnp.float32)
        else:
            total[start : start + count, :] += power.astype(jnp.float32)

    for harmonic in range(1, H + 1):
        build(harmonic)
        multiply(harmonic)
    out_ref[...] = total[:rows, :]


def harmonic_sums(slabs, picked, rows, sub_bins):
    filled = len(slabs) * slabs[0].shape[1] // LANES
    beyond = WIDTH // LANES + H * (sub_bins // LANES) + 1
    return pl.pallas_call(
        functools.partial(harmonic_kernel, n_slabs=len(slabs), rows=rows),
        out_shape=jax.ShapeDtypeStruct((rows, sub_bins), jnp.float32),
        in_specs=[VMEM] * (len(slabs) + 1),
        out_specs=VMEM,
        scratch_shapes=[
            pltpu.VMEM((2, filled + beyond, LANES), jnp.float32),
            pltpu.VMEM((H, 2, sub_bins, WIDTH), jnp.bfloat16),
            pltpu.VMEM((round_up(rows, 16), sub_bins), jnp.float32),
        ],
        compiler_params=pltpu.CompilerParams(vmem_limit_bytes=32 << 20),
        name="harmonic_sums",
    )(*slabs, picked)


def slab_steps(freq_count):
    ahead = list(range(freq_count - 1, 0, -1))
    return [(ahead[i], ahead[min(i + 1, len(ahead) - 1)]) for i in range(0, len(ahead), 2)]


def slab_slots(freq_count):
    steps = slab_steps(freq_count)
    return steps + [(odd, even) for even, odd in steps if even != odd] + [(0, 0)]


def swapped(value, mask):
    return lax.ppermute(value, "acc", [(i, i ^ mask) for i in range(lax.axis_size("acc"))])


def gathered_slabs(spectrum):
    freq_count, acc_count = lax.axis_size("freq"), lax.axis_size("acc")
    fetched = []
    for step in slab_steps(freq_count):
        pairs = [
            ((i + step[a % 2]) % freq_count * acc_count + a, i * acc_count + a)
            for i in range(freq_count)
            for a in range(acc_count)
            if i + step[a % 2] < freq_count
        ]
        fetched.append(lax.ppermute(spectrum, ("freq", "acc"), pairs))
    return fetched + [swapped(slab, 1) for slab, step in zip(fetched, slab_steps(freq_count)) if step[0] != step[1]] + [spectrum]


def gathered_templates(packed):
    return [shift_own(packed)] + [swapped(packed, mask) for mask in range(lax.axis_size("acc") - 1, 0, -1)]


def shards(spectrum, templates, offsets):
    acc_count = lax.axis_size("acc")
    rows = acc_count * templates.shape[1]
    slabs = gathered_slabs(spectrum)
    held = gathered_templates(pack_templates(jnp.transpose(templates, (1, 0, 2)), offsets))
    picked = pick_templates(held, [0, *range(acc_count - 1, 0, -1)], rows)
    return harmonic_sums(slabs, picked, rows, spectrum.shape[1] // acc_count)


def solution(mesh):
    return jax.shard_map(
        shards,
        mesh=mesh,
        in_specs=(P(None, ("trial", "freq")), P(None, "acc", None), P("acc")),
        out_specs=P(None, ("trial", "freq", "acc")),
        check_vma=False,
    )
```
